32 devices in a mesh: rep: 2 (over y), sec: 16 (over z, x, core).
Axes of the slice: x: 2, y: 2, z: 4, core: 2. Of those that a mesh axis runs over, the one named last changes fastest.
Arguments:
- wavefunction: bfloat16 [32, 312, 312], P(('rep', 'sec')), parts along dimension 0, may hold values from -21 to 21
- left_blocks: bfloat16 [28, 32, 312, 312], P(None, ('rep', 'sec')), parts along dimension 1, may hold values from -0.26 to 0.56
- right_blocks: bfloat16 [28, 32, 312, 312], P(None, ('rep', 'sec')), parts along dimension 1, may hold values from -0.0505 to 0.111
- diagonal: float32 [128, 78, 312], P(('rep', 'sec')), parts along dimension 0, may hold values from 0.5 to 6
- target_sector: int32 [56, 16], P('rep'), parts along dimension 0, may hold values from 0 to 15, as said below
- slot_sector: int32 [32], P('rep'), parts along dimension 0, may hold values from 0 to 15, as said below
- widths: int32 [32], P('rep'), parts along dimension 0, may hold values from 64 to 312, as said below
Outputs:
- residual: bfloat16 [128, 78, 312], P(('rep', 'sec')), parts along dimension 0
- quotient: float32 [2], P('rep'), parts along dimension 0
The draws below stay inside these ranges and needn't reach their ends.
There are 2 independent parts, one for each index of `rep`. The reference program is written for one: setup_inputs(seed, part) draws one part's arguments, and reference() takes and returns one part's arrays. A program takes and returns all parts, laid end to end along the dimension named above; each array names one. Nothing has to cross between parts.
Inputs may be any that keep to these rules, and one draw needn't show every extreme that they name: `slot_sector`: a permutation: each sector is held by exactly one slot. `target_sector`: for each term a permutation of the sectors; slots form groups of 4 consecutive indices; for every source slot the terms that lead its sector into one group number at most 8, into its own group at most 7, and every source slot reaches that bound in its own group. `widths`: both 64 and 312 occur.
All inputs are finite; a program needn't handle non-finite values.
Results may differ from the reference program's by a relative error of at most 0.0047.
Values may be sent and summed in bfloat16 or wider, within the bound.
A program may use at most 128 MiB of HBM per device.

```python
import jax
import jax.numpy as jnp
from jax import lax

W = 312
MINW = 64
PIECES = 4
NT = 28
NSEC = 16


def pairing(key):
    sector_key, offset_key, group_key, place_key = jax.random.split(key, 4)
    positions = jnp.arange(NSEC, dtype=jnp.int32)
    group_count = NSEC // PIECES
    bound = (NT + group_count) // group_count
    slot_sector = jax.random.permutation(sector_key, positions)
    order = jax.random.permutation(offset_key, jnp.arange(NT, dtype=jnp.int32))
    offsets = (order + 1) // bound
    group_order = jax.random.permutation(group_key, jnp.arange(group_count, dtype=jnp.int32))
    place_of = jnp.zeros((group_count,), jnp.int32).at[group_order].set(jnp.arange(group_count, dtype=jnp.int32))
    within = jax.vmap(lambda one_key: jax.random.permutation(one_key, jnp.arange(PIECES, dtype=jnp.int32)))(jax.random.split(place_key, NT))
    source_group = place_of[positions // PIECES]
    moved_group = group_order[(source_group[None, :] + offsets[:, None]) % group_count]
    moved_place = jnp.take_along_axis(within, jnp.broadcast_to((positions % PIECES)[None, :], (NT, NSEC)), axis=1)
    target_slot = moved_group * PIECES + moved_place
    target_sector = jnp.zeros((NT, NSEC), jnp.int32).at[:, slot_sector].set(slot_sector[target_slot])
    return (slot_sector.astype(jnp.int32), target_sector.astype(jnp.int32))


def row_levels(key):
    return jax.random.uniform(jax.random.fold_in(key, 11), (NSEC, W), jnp.float32)


def draw_slot_sector(key, part):
    return pairing(key)[0]


def draw_target_sector(key, part):
    return pairing(key)[1]


def draw_widths(key, part):
    key = jax.random.fold_in(key, 5)
    width_key, first_key, second_key = jax.random.split(key, 3)
    drawn = jax.random.randint(width_key, (NSEC,), MINW, W + 1)
    widest = jax.random.randint(first_key, (), 0, NSEC)
    narrow = (widest + 1 + jax.random.randint(second_key, (), 0, NSEC - 1)) % NSEC
    return drawn.at[widest].set(W).at[narrow].set(MINW).astype(jnp.int32)


def draw_wavefunction(key, part):
    shared_rows = row_levels(key)
    key = jax.random.fold_in(key, 7)
    value_key = jax.random.fold_in(key, 0)
    common_key = jax.random.fold_in(key, 2)
    rising = 1.0 + 2.0 * jnp.arange(W, dtype=jnp.float32) / (W - 1)
    row_factor = jnp.exp(0.7 * (shared_rows - 0.5))
    own_part = jax.random.normal(value_key, (NSEC, W, W), jnp.float32)
    common = jax.random.normal(common_key, (W, W), jnp.float32)
    values = jnp.clip(0.632 * common[None, :, :] + 0.775 * own_part, -4.0, 4.0)
    return (values * row_factor[:, :, None] * rising[None, :, None]).astype(jnp.bfloat16)


def draw_diagonal(key, part):
    shared_rows = row_levels(key)
    key = jax.random.fold_in(key, 9)
    levels = 1.0 + shared_rows
    levels = jnp.reshape(jnp.transpose(jnp.reshape(levels, (NSEC, PIECES, W // PIECES)), (1, 0, 2)), (PIECES * NSEC, W // PIECES))
    entry_ids = jnp.arange(PIECES * NSEC, dtype=jnp.int32)
    row_ids = (entry_ids // NSEC)[:, None] * (W // PIECES) + jnp.arange(W // PIECES, dtype=jnp.int32)[None, :]
    rising = 1.0 + 2.0 * row_ids.astype(jnp.float32) / (W - 1)
    base_part = jax.random.uniform(key, (PIECES * NSEC, W // PIECES, W), jnp.float32, 0.5, 1.0)
    return (base_part * (levels * rising)[:, :, None]).astype(jnp.float32)


def operator_blocks(key, deviation, diagonal_weight, limit):
    random_part = jax.random.normal(key, (NT, NSEC, W, W), jnp.float32) * deviation
    random_part = jnp.clip(random_part, -limit, limit)
    identity = jnp.eye(W, dtype=jnp.float32)
    return (random_part + diagonal_weight * identity[None, None, :, :]).astype(jnp.bfloat16)


def draw_left_blocks(key, part):
    key = jax.random.fold_in(key, 13)
    return operator_blocks(key, float(W) ** (-0.5), 0.3, 0.25)


def draw_right_blocks(key, part):
    key = jax.random.fold_in(key, 17)
    return operator_blocks(key, float(W * NT) ** (-0.5), 0.06, 0.05)


def setup_inputs(seed: int = 0, part: int = 0) -> dict:
    arg_keys = jax.random.split(jax.random.key(seed), 8)
    part_splits = jax.random.split(jax.random.fold_in(arg_keys[7], part), 8)
    wavefunction = draw_wavefunction(jax.random.fold_in(jax.random.fold_in(arg_keys[7], part), 71), part)
    left_blocks = draw_left_blocks(jax.random.fold_in(jax.random.fold_in(arg_keys[7], part), 71), part)
    right_blocks = draw_right_blocks(jax.random.fold_in(jax.random.fold_in(arg_keys[7], part), 71), part)
    diagonal = draw_diagonal(jax.random.fold_in(jax.random.fold_in(arg_keys[7], part), 71), part)
    target_sector = draw_target_sector(jax.random.fold_in(jax.random.fold_in(arg_keys[7], part), 71), part)
    slot_sector = draw_slot_sector(jax.random.fold_in(jax.random.fold_in(arg_keys[7], part), 71), part)
    widths = draw_widths(jax.random.fold_in(jax.random.fold_in(arg_keys[7], part), 71), part)
    return dict(wavefunction=wavefunction, left_blocks=left_blocks, right_blocks=right_blocks, diagonal=diagonal, target_sector=target_sector, slot_sector=slot_sector, widths=widths)


def reference(wavefunction, left_blocks, right_blocks, diagonal, target_sector, slot_sector, widths):
    positions = jnp.arange(NSEC, dtype=jnp.int32)
    slot_of = jnp.zeros((NSEC,), jnp.int32).at[slot_sector].set(positions)
    targets = slot_of[target_sector[:, slot_sector]].astype(jnp.int32)
    live_width = widths[slot_sector]
    keep_rows = jnp.arange(W, dtype=jnp.int32)[None, :] < live_width[:, None]
    live_box = jnp.logical_and(keep_rows[:, :, None], keep_rows[:, None, :])
    live_block = wavefunction * live_box.astype(wavefunction.dtype)
    live_float = live_block.astype(jnp.float32)

    def add_term(running, term_slices):
        left_block, right_block, target = term_slices
        half_done = jnp.einsum('sij,sjk->sik', left_block.astype(jnp.float32), live_float).astype(jnp.bfloat16)
        finished = jnp.einsum('sik,slk->sil', half_done.astype(jnp.float32), right_block.astype(jnp.float32)).astype(jnp.bfloat16)
        return running.at[target].add(finished.astype(jnp.float32)), None

    applied, _ = lax.scan(add_term, jnp.zeros((NSEC, W, W), jnp.float32), (left_blocks, right_blocks, targets))
    diag_full = jnp.transpose(jnp.reshape(diagonal, (PIECES, NSEC, W // PIECES, W)), (1, 0, 2, 3))
    diag_full = jnp.reshape(diag_full, (NSEC, W, W))
    product = diag_full * live_float + applied
    correlation = jnp.sum(live_float * product)
    squares = jnp.sum(live_float * live_float)
    quotient = correlation / squares
    full_residual = ((product - quotient * live_float) * live_box.astype(jnp.float32)).astype(jnp.bfloat16)
    residual = jnp.transpose(jnp.reshape(full_residual, (NSEC, PIECES, W // PIECES, W)), (1, 0, 2, 3))
    residual = jnp.reshape(residual, (PIECES * NSEC, W // PIECES, W))
    return residual, jnp.reshape(quotient, (1,)).astype(jnp.float32)
```

```python
import functools

import jax
import jax.numpy as jnp
from jax import lax
from jax.experimental import pallas as pl
from jax.experimental.pallas import tpu as pltpu
from jax.sharding import PartitionSpec as P

PIECES = 4
MESH = pl.DeviceIdType.MESH


def earlier_same(labels):
    count = labels.shape[-1]
    same_label = labels[..., :, None] == labels[..., None, :]
    earlier = jnp.arange(count)[None, :] < jnp.arange(count)[:, None]
    return jnp.sum(jnp.logical_and(same_label, earlier).astype(jnp.int32), axis=-1)


def gathered_shards(wavefunction, left_blocks, right_blocks, diagonal, target_sector, slot_sector, widths):
    owners = lax.axis_size("sec")
    own_index = lax.axis_index("sec")
    term_count = left_blocks.shape[0]
    block_width = wavefunction.shape[1]
    piece_rows = block_width // PIECES
    groups = owners // PIECES
    capacity = (term_count + groups) // groups
    item_count = term_count + 1
    positions = jnp.arange(owners, dtype=jnp.int32)
    slot_of = jnp.zeros((owners,), jnp.int32).at[slot_sector].set(positions)
    targets = slot_of[target_sector[:, slot_sector]]
    live_width = widths[slot_sector]
    column_ids = jnp.arange(block_width, dtype=jnp.int32)
    own_keep = column_ids < live_width[own_index]
    live_block = wavefunction[0] * jnp.logical_and(own_keep[:, None], own_keep[None, :]).astype(
        wavefunction.dtype
    )
    item_slots = jnp.concatenate([jnp.reshape(own_index, (1,)), targets[:, own_index]])
    item_groups = item_slots // PIECES
    item_rank = earlier_same(item_groups)
    destination = jnp.arange(PIECES, dtype=jnp.int32)[None, :] * groups + item_groups[:, None]
    rank_grid = jnp.broadcast_to(item_rank[:, None], (item_count, PIECES))
    half_done = jnp.einsum(
        "tij,jk->tik", left_blocks[:, 0], live_block, preferred_element_type=jnp.float32
    ).astype(jnp.bfloat16)
    term_blocks = jnp.einsum(
        "tik,tlk->til", half_done, right_blocks[:, 0], preferred_element_type=jnp.float32
    ).astype(jnp.bfloat16)
    pieces = jnp.reshape(
        jnp.concatenate([live_block[None], term_blocks]),
        (item_count, PIECES, piece_rows, block_width),
    )
    outgoing = (
        jnp.zeros((owners, capacity, piece_rows, block_width), jnp.bfloat16)
        .at[destination, rank_grid]
        .set(pieces)
    )
    received = lax.all_to_all(outgoing, "sec", split_axis=0, concat_axis=0, tiled=True)
    my_piece = own_index // groups
    my_group = own_index % groups
    all_slots = jnp.concatenate([positions[:, None], jnp.transpose(targets)], axis=1)
    all_groups = all_slots // PIECES
    all_rank = earlier_same(all_groups)
    is_mine = all_groups == my_group
    rank_hit = jnp.logical_and(
        all_rank[:, :, None] == jnp.arange(capacity, dtype=jnp.int32)[None, None, :],
        is_mine[:, :, None],
    )
    place_hit = (
        (all_slots % PIECES)[:, :, None] == jnp.arange(PIECES, dtype=jnp.int32)[None, None, :]
    ).astype(jnp.float32)
    is_live = (jnp.arange(item_count) == 0)[None, :, None]
    live_weight = jnp.einsum(
        "smc,smp->scp", jnp.logical_and(rank_hit, is_live).astype(jnp.float32), place_hit
    )
    term_weight = jnp.einsum(
        "smc,smp->scp",
        jnp.logical_and(rank_hit, jnp.logical_not(is_live)).astype(jnp.float32),
        place_hit,
    )
    live_pieces = jnp.einsum(
        "scp,scab->pab",
        live_weight.astype(jnp.bfloat16),
        received,
        preferred_element_type=jnp.float32,
    )
    applied = jnp.einsum(
        "scp,scab->pab",
        term_weight.astype(jnp.bfloat16),
        received,
        preferred_element_type=jnp.float32,
    )
    my_slots = my_group * PIECES + jnp.arange(PIECES, dtype=jnp.int32)
    widths_here = live_width[my_slots]
    row_global = my_piece * piece_rows + jnp.arange(piece_rows, dtype=jnp.int32)
    keep_piece_rows = row_global[None, :] < widths_here[:, None]
    keep_piece_cols = column_ids[None, :] < widths_here[:, None]
    piece_box = jnp.logical_and(keep_piece_rows[:, :, None], keep_piece_cols[:, None, :]).astype(
        jnp.float32
    )
    product = diagonal * live_pieces + applied
    correlation_local = jnp.sum(live_pieces * product)
    correlation, squares = lax.psum((correlation_local, jnp.sum(live_pieces * live_pieces)), "sec")
    quotient = correlation / squares
    residual = ((product - quotient * live_pieces) * piece_box).astype(jnp.bfloat16)
    return (residual, jnp.reshape(quotient, (1,)))


def round_up(value, unit):
    return (value + unit - 1) // unit * unit


def local_kernel(
    slot_sector, target_sector, widths, wave, left, right, out, live_out,
    slot_of, lbuf, rbuf, acc, lsem, rsem,
):
    terms, width = lbuf.shape[0], lbuf.shape[1]
    owners = slot_sector.shape[0]
    me = lax.axis_index("sec")
    rows = width // PIECES
    main = width // 128 * 128
    rest = width - main

    @pl.loop(0, terms)
    def _(t):
        pltpu.make_async_copy(left.at[t], lbuf.at[t], lsem.at[t]).start()
        pltpu.make_async_copy(right.at[t], rbuf.at[t], rsem.at[t]).start()

    @pl.loop(0, owners)
    def _(d):
        slot_of[slot_sector[d]] = d

    @pl.loop(0, owners)
    def _(d):
        acc[d] = jnp.zeros(acc.shape[1:], acc.dtype)

    sector = slot_sector[me]
    own_width = widths[sector]
    row_ids = lax.broadcasted_iota(jnp.int32, (width, width), 0)
    column_ids = lax.broadcasted_iota(jnp.int32, (width, width), 1)
    keep = jnp.logical_and(row_ids < own_width, column_ids < own_width)
    live_wide = jnp.where(keep, wave[0].astype(jnp.float32), 0.0)
    live = live_wide.astype(jnp.bfloat16)
    for p in range(PIECES):
        piece = live_wide[p * rows : (p + 1) * rows].astype(jnp.bfloat16)
        live_out[p, :rows, :width] = piece

    batch = 4

    @pl.loop(0, terms // batch)
    def _(step):
        for b in range(batch):
            t = step * batch + b
            pltpu.make_async_copy(left.at[t], lbuf.at[t], lsem.at[t]).wait()
            pltpu.make_async_copy(right.at[t], rbuf.at[t], rsem.at[t]).wait()
        blocks = []
        for b in range(batch):
            t = step * batch + b
            half = jnp.dot(lbuf[t], live, preferred_element_type=jnp.float32)
            blocks.append(
                lax.dot_general(
                    half.astype(jnp.bfloat16), rbuf[t], (((1,), (1,)), ((), ())),
                    preferred_element_type=jnp.float32,
                )
            )
        for b in range(batch):
            v = slot_of[target_sector[step * batch + b, sector]]
            acc[v] += blocks[b]

    pad = jnp.zeros((rows, out.shape[-1] - 2 * width), jnp.float32)

    @pl.loop(0, owners // 2)
    def _(pair):
        for p in range(PIECES):
            even = acc[2 * pair, p * rows : (p + 1) * rows, :]
            odd = acc[2 * pair + 1, p * rows : (p + 1) * rows, :]
            packed = jnp.concatenate(
                [even[:, :main], odd[:, :main], even[:, main:], odd[:, main:], pad], axis=1
            )
            out[pair // 2, 2 * p + pair % 2, :rows, :] = packed.astype(out.dtype)


def reduce_kernel(
    slot_sector, widths, sums, live_pieces, diagonal, residual, quotient,
    own, crecv, xrecv, zrecv, lives, diag, product, stats, stats_all,
    own_sem, diag_sem, self_sem, csend_sem, crecv_sem, xsend_sem, xrecv_sem, zsend_sem, zrecv_sem,
    lsend_sem, lrecv_sem, ssend_sem, srecv_sem,
):
    rep = lax.axis_index("rep")
    me = lax.axis_index("sec")
    owners = slot_sector.shape[0]
    z, x, c = me // 4, (me // 2) % 2, me % 2
    group = me % 4
    units = 2 * PIECES
    rows, width = diag.shape[1], diag.shape[2]
    main = width // 128 * 128
    rest = width - main
    far, near = (1 - x) * 2, x * 2

    def unit_of(i):
        return ((z + 1 + i // 2) % PIECES) * 2 + i % 2

    def core_copy(which, u):
        source_group = (far if which == 0 else near) + (1 - c)
        return pltpu.make_async_remote_copy(
            src_ref=sums.at[source_group, u], dst_ref=crecv.at[which, u],
            send_sem=csend_sem.at[which, u], recv_sem=crecv_sem.at[which, u],
            device_id=(rep, near + z * 4 + (1 - c)), device_id_type=MESH,
        )

    def x_copy(u):
        return pltpu.make_async_remote_copy(
            src_ref=own.at[0, u], dst_ref=xrecv.at[u],
            send_sem=xsend_sem.at[u], recv_sem=xrecv_sem.at[u],
            device_id=(rep, z * 4 + far + c), device_id_type=MESH,
        )

    def z_copy(u, source_z):
        q = u % 2
        return pltpu.make_async_remote_copy(
            src_ref=own.at[1, u], dst_ref=zrecv.at[source_z, q],
            send_sem=zsend_sem.at[u], recv_sem=zrecv_sem.at[source_z, q],
            device_id=(rep, (u // 2) * 4 + group), device_id_type=MESH,
        )

    def live_copy(p, place):
        return pltpu.make_async_remote_copy(
            src_ref=live_pieces.at[p], dst_ref=lives.at[place],
            send_sem=lsend_sem.at[p], recv_sem=lrecv_sem.at[place],
            device_id=(rep, p * 4 + z), device_id_type=MESH,
        )

    def stats_copy(other, source):
        return pltpu.make_async_remote_copy(
            src_ref=stats, dst_ref=stats_all.at[source],
            send_sem=ssend_sem.at[other], recv_sem=srecv_sem.at[source],
            device_id=(rep, other), device_id_type=MESH,
        )

    own_far = pltpu.make_async_copy(sums.at[far + c], own.at[0], own_sem.at[0])
    own_near = pltpu.make_async_copy(sums.at[near + c], own.at[1], own_sem.at[1])
    own_far.start()
    own_near.start()
    diag_copy = pltpu.make_async_copy(diagonal, diag, diag_sem)
    diag_copy.start()

    barrier = pltpu.get_barrier_semaphore()

    @pl.loop(1, owners)
    def _(d):
        pl.semaphore_signal(
            barrier, inc=1, device_id=(rep, (me + d) % owners), device_id_type=MESH
        )

    pl.semaphore_wait(barrier, owners - 1)

    @pl.loop(0, units)
    def _(i):
        core_copy(0, unit_of(i)).start()

    @pl.loop(0, units)
    def _(i):
        core_copy(1, unit_of(i)).start()

    self_copy = pltpu.make_async_copy(live_pieces.at[z], lives.at[group], self_sem)
    for p in range(PIECES):

        @pl.when(p * 4 + z != me)
        def _():
            live_copy(p, group).start()

        @pl.when(p * 4 + z == me)
        def _():
            self_copy.start()

    own_far.wait()

    @pl.loop(0, units)
    def _(i):
        u = unit_of(i)
        core_copy(0, u).wait_recv()
        total = own[0, u].astype(jnp.float32) + crecv[0, u].astype(jnp.float32)
        own[0, u] = total.astype(own.dtype)
        x_copy(u).start()

    own_near.wait()

    @pl.loop(0, units - 2)
    def _(i):
        u = unit_of(i)
        core_copy(1, u).wait_recv()
        x_copy(u).wait_recv()
        total = own[1, u].astype(jnp.float32) + crecv[1, u].astype(jnp.float32)
        total += xrecv[u].astype(jnp.float32)
        own[1, u] = total.astype(own.dtype)
        z_copy(u, z).start()

    for j in range(PIECES):
        source = group * 4 + j

        @pl.when(source != me)
        def _():
            live_copy(0, j).wait_recv()

        @pl.when(source == me)
        def _():
            self_copy.wait()

    diag_copy.wait()

    correlation = jnp.zeros((1, width), jnp.float32)
    squares = jnp.zeros((1, width), jnp.float32)
    for q in range(2):
        u = z * 2 + q
        core_copy(1, u).wait_recv()
        x_copy(u).wait_recv()
        total = own[1, u].astype(jnp.float32) + crecv[1, u].astype(jnp.float32)
        total += xrecv[u].astype(jnp.float32)
        for d in range(1, PIECES):
            source_z = (z + d) % PIECES
            z_copy(q, source_z).wait_recv()
            total += zrecv[source_z, q].astype(jnp.float32)
        total = total[:rows]
        tail = 2 * main
        for parity in range(2):
            j = 2 * q + parity
            applied = jnp.concatenate(
                [
                    total[:, parity * main : (parity + 1) * main],
                    total[:, tail + parity * rest : tail + (parity + 1) * rest],
                ],
                axis=1,
            )
            live = lives[j, :rows, :width].astype(jnp.float32)
            block = diag[j] * live + applied
            product[j] = block
            correlation += jnp.sum(live * block, axis=0, keepdims=True)
            squares += jnp.sum(live * live, axis=0, keepdims=True)

    row_ids = lax.broadcasted_iota(jnp.int32, stats.shape, 0)
    mine = jnp.where(row_ids == 0, jnp.sum(correlation), jnp.sum(squares))
    stats[...] = mine
    stats_all[me] = mine

    @pl.loop(1, owners)
    def _(d):
        stats_copy((me + d) % owners, me).start()

    @pl.loop(1, owners)
    def _(d):
        stats_copy(me, (me + d) % owners).wait_recv()

    whole = stats_all[0]
    for d in range(1, owners):
        whole += stats_all[d]
    ratio = whole[0:1, 0:1] / whole[1:2, 0:1]
    quotient[...] = jnp.broadcast_to(ratio, quotient.shape)
    row_ids = lax.broadcasted_iota(jnp.int32, (rows, width), 0) + z * rows
    column_ids = lax.broadcasted_iota(jnp.int32, (rows, width), 1)
    for j in range(PIECES):
        slot_width = widths[slot_sector[group * 4 + j]]
        keep = jnp.logical_and(row_ids < slot_width, column_ids < slot_width)
        live = lives[j, :rows, :width].astype(jnp.float32)
        value = jnp.where(keep, product[j] - ratio * live, 0.0)
        residual[j] = value.astype(residual.dtype)

    @pl.loop(0, units)
    def _(u):
        core_copy(0, u).wait_send()
        core_copy(1, u).wait_send()
        x_copy(u).wait_send()

    @pl.loop(0, units - 2)
    def _(i):
        z_copy(unit_of(i), z).wait_send()

    for p in range(PIECES):

        @pl.when(p * 4 + z != me)
        def _():
            live_copy(p, group).wait_send()

    @pl.loop(1, owners)
    def _(d):
        stats_copy((me + d) % owners, me).wait_send()


def kernel_shards(
    wavefunction, left_blocks, right_blocks, diagonal, target_sector, slot_sector, widths
):
    terms, _, width, _ = left_blocks.shape
    owners = slot_sector.shape[0]
    rows = width // PIECES
    groups = owners // PIECES
    units = 2 * PIECES
    tall = round_up(rows, 16)
    lanes = round_up(width, 128)
    packed = round_up(2 * width, 128)
    smem = pl.BlockSpec(memory_space=pltpu.SMEM)
    vmem = pl.BlockSpec(memory_space=pltpu.VMEM)
    hbm = pl.BlockSpec(memory_space=pl.ANY)
    sums, live_pieces = pl.pallas_call(
        local_kernel,
        out_shape=(
            jax.ShapeDtypeStruct((groups, units, tall, packed), jnp.bfloat16),
            jax.ShapeDtypeStruct((PIECES, tall, lanes), jnp.bfloat16),
        ),
        in_specs=[smem, smem, smem, vmem, hbm, hbm],
        out_specs=(vmem, vmem),
        scratch_shapes=[
            pltpu.SMEM((owners,), jnp.int32),
            pltpu.VMEM((terms, width, width), jnp.bfloat16),
            pltpu.VMEM((terms, width, width), jnp.bfloat16),
            pltpu.VMEM((owners, width, width), jnp.float32),
            pltpu.SemaphoreType.DMA((terms,)),
            pltpu.SemaphoreType.DMA((terms,)),
        ],
        compiler_params=pltpu.CompilerParams(vmem_limit_bytes=48 << 20),
        name="local_sums",
    )(slot_sector, target_sector, widths, wavefunction, left_blocks[:, 0], right_blocks[:, 0])
    block = (tall, packed)
    dma = pltpu.SemaphoreType.DMA
    residual, quotient = pl.pallas_call(
        reduce_kernel,
        out_shape=(
            jax.ShapeDtypeStruct((PIECES, rows, width), jnp.bfloat16),
            jax.ShapeDtypeStruct((1, 1), jnp.float32),
        ),
        in_specs=[smem, smem, hbm, hbm, hbm],
        out_specs=(vmem, vmem),
        scratch_shapes=[
            pltpu.VMEM((2, units, *block), jnp.bfloat16),
            pltpu.VMEM((2, units, *block), jnp.bfloat16),
            pltpu.VMEM((units, *block), jnp.bfloat16),
            pltpu.VMEM((PIECES, 2, *block), jnp.bfloat16),
            pltpu.VMEM((PIECES, tall, lanes), jnp.bfloat16),
            pltpu.VMEM((PIECES, rows, width), jnp.float32),
            pltpu.VMEM((PIECES, rows, width), jnp.float32),
            pltpu.VMEM((8, 128), jnp.float32),
            pltpu.VMEM((owners, 8, 128), jnp.float32),
            dma((2,)), dma, dma,
            dma((2, units)), dma((2, units)), dma((units,)), dma((units,)),
            dma((units,)), dma((PIECES, 2)),
            dma((PIECES,)), dma((PIECES,)), dma((owners,)), dma((owners,)),
        ],
        compiler_params=pltpu.CompilerParams(
            collective_id=0, has_side_effects=True, vmem_limit_bytes=48 << 20
        ),
        name="reduce_pieces",
    )(slot_sector, widths, sums, live_pieces, diagonal)
    return residual, jnp.reshape(quotient, (1,))


def solution(mesh):
    in_specs = (
        P(("rep", "sec"), None, None),
        P(None, ("rep", "sec"), None, None),
        P(None, ("rep", "sec"), None, None),
        P(("rep", "sec"), None, None),
        P("rep", None),
        P("rep"),
        P("rep"),
    )
    out_specs = (P(("rep", "sec"), None, None), P("rep"))
    fast = mesh.shape["sec"] == PIECES * 4
    shards = kernel_shards if fast else gathered_shards
    return jax.shard_map(shards, mesh=mesh, in_specs=in_specs, out_specs=out_specs, check_vma=False)
```

```python
import functools

import jax
import jax.numpy as jnp
from jax import lax
from jax.experimental import pallas as pl
from jax.experimental.pallas import tpu as pltpu
from jax.sharding import PartitionSpec as P

PIECES = 4
MESH = pl.DeviceIdType.MESH


def earlier_same(labels):
    count = labels.shape[-1]
    same_label = labels[..., :, None] == labels[..., None, :]
    earlier = jnp.arange(count)[None, :] < jnp.arange(count)[:, None]
    return jnp.sum(jnp.logical_and(same_label, earlier).astype(jnp.int32), axis=-1)


def gathered_shards(wavefunction, left_blocks, right_blocks, diagonal, target_sector, slot_sector, widths):
    owners = lax.axis_size("sec")
    own_index = lax.axis_index("sec")
    term_count = left_blocks.shape[0]
    block_width = wavefunction.shape[1]
    piece_rows = block_width // PIECES
    groups = owners // PIECES
    capacity = (term_count + groups) // groups
    item_count = term_count + 1
    positions = jnp.arange(owners, dtype=jnp.int32)
    slot_of = jnp.zeros((owners,), jnp.int32).at[slot_sector].set(positions)
    targets = slot_of[target_sector[:, slot_sector]]
    live_width = widths[slot_sector]
    column_ids = jnp.arange(block_width, dtype=jnp.int32)
    own_keep = column_ids < live_width[own_index]
    live_block = wavefunction[0] * jnp.logical_and(own_keep[:, None], own_keep[None, :]).astype(
        wavefunction.dtype
    )
    item_slots = jnp.concatenate([jnp.reshape(own_index, (1,)), targets[:, own_index]])
    item_groups = item_slots // PIECES
    item_rank = earlier_same(item_groups)
    destination = jnp.arange(PIECES, dtype=jnp.int32)[None, :] * groups + item_groups[:, None]
    rank_grid = jnp.broadcast_to(item_rank[:, None], (item_count, PIECES))
    half_done = jnp.einsum(
        "tij,jk->tik", left_blocks[:, 0], live_block, preferred_element_type=jnp.float32
    ).astype(jnp.bfloat16)
    term_blocks = jnp.einsum(
        "tik,tlk->til", half_done, right_blocks[:, 0], preferred_element_type=jnp.float32
    ).astype(jnp.bfloat16)
    pieces = jnp.reshape(
        jnp.concatenate([live_block[None], term_blocks]),
        (item_count, PIECES, piece_rows, block_width),
    )
    outgoing = (
        jnp.zeros((owners, capacity, piece_rows, block_width), jnp.bfloat16)
        .at[destination, rank_grid]
        .set(pieces)
    )
    received = lax.all_to_all(outgoing, "sec", split_axis=0, concat_axis=0, tiled=True)
    my_piece = own_index // groups
    my_group = own_index % groups
    all_slots = jnp.concatenate([positions[:, None], jnp.transpose(targets)], axis=1)
    all_groups = all_slots // PIECES
    all_rank = earlier_same(all_groups)
    is_mine = all_groups == my_group
    rank_hit = jnp.logical_and(
        all_rank[:, :, None] == jnp.arange(capacity, dtype=jnp.int32)[None, None, :],
        is_mine[:, :, None],
    )
    place_hit = (
        (all_slots % PIECES)[:, :, None] == jnp.arange(PIECES, dtype=jnp.int32)[None, None, :]
    ).astype(jnp.float32)
    is_live = (jnp.arange(item_count) == 0)[None, :, None]
    live_weight = jnp.einsum(
        "smc,smp->scp", jnp.logical_and(rank_hit, is_live).astype(jnp.float32), place_hit
    )
    term_weight = jnp.einsum(
        "smc,smp->scp",
        jnp.logical_and(rank_hit, jnp.logical_not(is_live)).astype(jnp.float32),
        place_hit,
    )
    live_pieces = jnp.einsum(
        "scp,scab->pab",
        live_weight.astype(jnp.bfloat16),
        received,
        preferred_element_type=jnp.float32,
    )
    applied = jnp.einsum(
        "scp,scab->pab",
        term_weight.astype(jnp.bfloat16),
        received,
        preferred_element_type=jnp.float32,
    )
    my_slots = my_group * PIECES + jnp.arange(PIECES, dtype=jnp.int32)
    widths_here = live_width[my_slots]
    row_global = my_piece * piece_rows + jnp.arange(piece_rows, dtype=jnp.int32)
    keep_piece_rows = row_global[None, :] < widths_here[:, None]
    keep_piece_cols = column_ids[None, :] < widths_here[:, None]
    piece_box = jnp.logical_and(keep_piece_rows[:, :, None], keep_piece_cols[:, None, :]).astype(
        jnp.float32
    )
    product = diagonal * live_pieces + applied
    correlation_local = jnp.sum(live_pieces * product)
    correlation, squares = lax.psum((correlation_local, jnp.sum(live_pieces * live_pieces)), "sec")
    quotient = correlation / squares
    residual = ((product - quotient * live_pieces) * piece_box).astype(jnp.bfloat16)
    return (residual, jnp.reshape(quotient, (1,)))


def round_up(value, unit):
    return (value + unit - 1) // unit * unit


def to_column(row, count):
    wide = jnp.broadcast_to(row[:, :count], (count, count))
    eye = lax.broadcasted_iota(jnp.int32, (count, count), 0) == lax.broadcasted_iota(
        jnp.int32, (count, count), 1
    )
    return jnp.sum(jnp.where(eye, wide, 0.0), axis=1, keepdims=True)


def make_plan(slot_row, target_rows, width_row, me):
    owners, terms = target_rows.shape
    slot_column = to_column(slot_row, owners)
    at_owner = lax.broadcasted_iota(jnp.int32, (owners, 1), 0)
    sector = jnp.sum(jnp.where(at_owner == me, slot_column, 0.0), axis=0, keepdims=True)
    target = jnp.sum(
        jnp.where(at_owner.astype(jnp.float32) == sector, target_rows, 0.0), axis=0, keepdims=True
    )
    owner_ids = at_owner.astype(jnp.float32)
    slot = jnp.sum(jnp.where(slot_column == target, owner_ids, 0.0), axis=0, keepdims=True)
    column = to_column(slot, terms)
    term_row = lax.broadcasted_iota(jnp.int32, (terms, terms), 1)
    term_column = lax.broadcasted_iota(jnp.int32, (terms, terms), 0)
    ahead = jnp.logical_or(
        slot < column, jnp.logical_and(slot == column, term_row < term_column)
    )
    rank = jnp.sum(jnp.where(ahead, 1.0, 0.0), axis=1, keepdims=True)
    lanes = lax.broadcasted_iota(jnp.int32, (terms, 128), 1).astype(jnp.float32)
    term_ids = lax.broadcasted_iota(jnp.int32, (terms, 128), 0).astype(jnp.float32)
    order = jnp.sum(jnp.where(rank == lanes, term_ids, 0.0), axis=0, keepdims=True)
    start = jnp.sum(jnp.where(column < lanes, 1.0, 0.0), axis=0, keepdims=True)
    width_column = to_column(width_row, owners)
    widths = jnp.sum(
        jnp.where(owner_ids == slot_row, width_column, 0.0), axis=0, keepdims=True
    )
    return order, start, widths


def fused_kernel(
    slot_sector, target_sector, widths, wave, left, right, diagonal, residual, quotient,
    slot_vmem, target_vmem, width_vmem, wave_vmem, plan_vmem, plan, lbuf, rbuf, running,
    own, crecv, xrecv, zrecv, live_pieces, lives, diag_raw, product, stats, stats_all,
    small_sem, plan_sem, lsem, rsem, diag_sem, self_sem,
    csend_sem, crecv_sem, xsend_sem, xrecv_sem, zsend_sem, zrecv_sem,
    lsend_sem, lrecv_sem, ssend_sem, srecv_sem,
):
    rep = lax.axis_index("rep")
    me = lax.axis_index("sec")
    owners = slot_sector.shape[1]
    terms, width = lbuf.shape[0], lbuf.shape[1]
    groups = owners // PIECES
    capacity = (terms + groups) // groups
    z, x, c = me // 4, (me // 2) % 2, me % 2
    group = me % 4
    units = 2 * PIECES
    rows = width // PIECES
    main = width // 128 * 128
    rest = width - main
    far, near = (1 - x) * 2, x * 2

    small = [
        pltpu.make_async_copy(source, target, small_sem.at[i])
        for i, (source, target) in enumerate(
            (
                (wave.at[0], wave_vmem),
                (slot_sector, slot_vmem),
                (target_sector, target_vmem),
                (widths, width_vmem),
            )
        )
    ]
    for copy in small:
        copy.start()

    @pl.loop(0, terms)
    def _(t):
        pltpu.make_async_copy(left.at[t], lbuf.at[t], lsem.at[t]).start()

    @pl.loop(0, terms)
    def _(t):
        pltpu.make_async_copy(right.at[t], rbuf.at[t], rsem.at[t]).start()

    diag_copy = pltpu.make_async_copy(diagonal, diag_raw, diag_sem)
    diag_copy.start()

    barrier = pltpu.get_barrier_semaphore()
    for d in range(1, owners):
        pl.semaphore_signal(
            barrier, inc=1, device_id=(rep, (me + d) % owners), device_id_type=MESH
        )

    for copy in small:
        copy.wait()
    order, start, slot_widths = make_plan(
        slot_vmem[...].astype(jnp.float32),
        target_vmem[...].astype(jnp.float32),
        width_vmem[...].astype(jnp.float32),
        me,
    )
    plan_vmem[0:1, :] = order.astype(jnp.int32)
    plan_vmem[1:2, :] = start.astype(jnp.int32)
    plan_copy = pltpu.make_async_copy(plan_vmem, plan, plan_sem)
    plan_copy.start()

    def width_of(slot):
        ids = lax.broadcasted_iota(jnp.int32, slot_widths.shape, 1)
        picked = jnp.sum(jnp.where(ids == slot, slot_widths, 0.0), axis=1, keepdims=True)
        return picked.astype(jnp.int32)

    own_width = width_of(me)
    row_ids = lax.broadcasted_iota(jnp.int32, (width, width), 0)
    column_ids = lax.broadcasted_iota(jnp.int32, (width, width), 1)
    keep = jnp.logical_and(row_ids < own_width, column_ids < own_width)
    live_wide = jnp.where(keep, wave_vmem[...].astype(jnp.float32), 0.0)
    live = live_wide.astype(jnp.bfloat16)
    for p in range(PIECES):
        piece = live_wide[p * rows : (p + 1) * rows].astype(jnp.bfloat16)
        live_pieces[p, :rows, :width] = piece

    def unit_of(i):
        return ((z + 1 + i // 2) % PIECES) * 2 + i % 2

    def core_copy(which, u):
        return pltpu.make_async_remote_copy(
            src_ref=own.at[2 * which, u], dst_ref=crecv.at[which, u],
            send_sem=csend_sem.at[which, u], recv_sem=crecv_sem.at[which, u],
            device_id=(rep, near + z * 4 + (1 - c)), device_id_type=MESH,
        )

    def x_copy(u):
        return pltpu.make_async_remote_copy(
            src_ref=own.at[1, u], dst_ref=xrecv.at[u],
            send_sem=xsend_sem.at[u], recv_sem=xrecv_sem.at[u],
            device_id=(rep, z * 4 + far + c), device_id_type=MESH,
        )

    def z_copy(u, source_z):
        q = u % 2
        return pltpu.make_async_remote_copy(
            src_ref=own.at[3, u], dst_ref=zrecv.at[source_z, q],
            send_sem=zsend_sem.at[u], recv_sem=zrecv_sem.at[source_z, q],
            device_id=(rep, (u // 2) * 4 + group), device_id_type=MESH,
        )

    def live_copy(p, place):
        return pltpu.make_async_remote_copy(
            src_ref=live_pieces.at[p], dst_ref=lives.at[place],
            send_sem=lsend_sem.at[p], recv_sem=lrecv_sem.at[place],
            device_id=(rep, p * 4 + z), device_id_type=MESH,
        )

    def stats_copy(level, other, source):
        device = z * 4 + other if level == 0 else other * 4 + group
        return pltpu.make_async_remote_copy(
            src_ref=stats.at[level], dst_ref=stats_all.at[level, source],
            send_sem=ssend_sem.at[level, other], recv_sem=srecv_sem.at[level, source],
            device_id=(rep, device), device_id_type=MESH,
        )

    batch = 4

    @pl.loop(0, terms // batch)
    def _(step):
        for b in range(batch):
            t = step * batch + b
            pltpu.make_async_copy(left.at[t], lbuf.at[t], lsem.at[t]).wait()
        for b in range(batch):
            t = step * batch + b
            half = jnp.dot(lbuf[t], live, preferred_element_type=jnp.float32)
            lbuf[t] = half.astype(jnp.bfloat16)

    pl.semaphore_wait(barrier, owners - 1)
    self_copy = pltpu.make_async_copy(live_pieces.at[z], lives.at[group], self_sem)
    for p in range(PIECES):

        @pl.when(p * 4 + z != me)
        def _():
            live_copy(p, group).start()

        @pl.when(p * 4 + z == me)
        def _():
            self_copy.start()

    running[0] = jnp.zeros((width, width), jnp.float32)
    plan_copy.wait()

    @pl.loop(0, terms)
    def _(t):
        pltpu.make_async_copy(right.at[t], rbuf.at[t], rsem.at[t]).wait()

    pad = jnp.zeros((rows, own.shape[-1] - 2 * width), jnp.float32)

    @pl.loop(0, groups)
    def _(k):
        target_group = jnp.where(k < 2, far, near) + jnp.where(k % 2 == 0, 1 - c, c)
        first = plan[1, target_group * PIECES]
        for i in range(capacity):
            t = jnp.clip(plan[0, jnp.clip(first + i, 0, terms - 1)], 0, terms - 1)
            term = lax.dot_general(
                lbuf[t], rbuf[t], (((1,), (1,)), ((), ())), preferred_element_type=jnp.float32
            )
            running[i + 1] = term if i == 0 else running[i] + term
        for q in range(2):
            ends = [
                jnp.clip(plan[1, target_group * PIECES + 2 * q + e] - first, 0, capacity)
                for e in range(3)
            ]
            for p in range(PIECES):
                at = slice(p * rows, (p + 1) * rows)
                low, middle, high = [running[end, at, :] for end in ends]
                even, odd = middle - low, high - middle
                packed = jnp.concatenate(
                    [even[:, :main], odd[:, :main], even[:, main:], odd[:, main:], pad], axis=1
                )
                own[k, 2 * p + q, :rows, :] = packed.astype(own.dtype)

        @pl.when(k % 2 == 0)
        def _():
            @pl.loop(0, units)
            def _(i):
                core_copy(k // 2, unit_of(i)).start()

        @pl.when(k == 1)
        def _():
            @pl.loop(0, units)
            def _(i):
                u = unit_of(i)
                core_copy(0, u).wait_recv()
                total = own[1, u].astype(jnp.float32) + crecv[0, u].astype(jnp.float32)
                own[1, u] = total.astype(own.dtype)
                x_copy(u).start()

    @pl.loop(0, units - 2)
    def _(i):
        u = unit_of(i)
        core_copy(1, u).wait_recv()
        x_copy(u).wait_recv()
        total = own[3, u].astype(jnp.float32) + crecv[1, u].astype(jnp.float32)
        total += xrecv[u].astype(jnp.float32)
        own[3, u] = total.astype(own.dtype)
        z_copy(u, z).start()

    for j in range(PIECES):
        source = group * 4 + j

        @pl.when(source != me)
        def _():
            live_copy(0, j).wait_recv()

        @pl.when(source == me)
        def _():
            self_copy.wait()

    diag_copy.wait()
    for j in range(PIECES):
        product[j] = diag_raw[:, j, :] * lives[j, :rows, :width].astype(jnp.float32)

    correlation = jnp.zeros((1, width), jnp.float32)
    squares = jnp.zeros((1, width), jnp.float32)
    for q in range(2):
        u = z * 2 + q
        core_copy(1, u).wait_recv()
        x_copy(u).wait_recv()
        total = own[3, u].astype(jnp.float32) + crecv[1, u].astype(jnp.float32)
        total += xrecv[u].astype(jnp.float32)
        for d in range(1, PIECES):
            source_z = (z + d) % PIECES
            z_copy(q, source_z).wait_recv()
            total += zrecv[source_z, q].astype(jnp.float32)
        total = total[:rows]
        tail = 2 * main
        for parity in range(2):
            j = 2 * q + parity
            applied = jnp.concatenate(
                [
                    total[:, parity * main : (parity + 1) * main],
                    total[:, tail + parity * rest : tail + (parity + 1) * rest],
                ],
                axis=1,
            )
            live = lives[j, :rows, :width].astype(jnp.float32)
            block = product[j] + applied
            product[j] = block
            correlation += jnp.sum(live * block, axis=0, keepdims=True)
            squares += jnp.sum(live * live, axis=0, keepdims=True)

    row_ids = lax.broadcasted_iota(jnp.int32, stats.shape[1:], 0)
    mine = jnp.where(row_ids == 0, jnp.sum(correlation), jnp.sum(squares))
    for level in range(2):
        here = group if level == 0 else z
        stats[level] = mine
        stats_all[level, here] = mine
        for d in range(1, PIECES):
            stats_copy(level, (here + d) % PIECES, here).start()
        for d in range(1, PIECES):
            stats_copy(level, here, (here + d) % PIECES).wait_recv()
        mine = stats_all[level, 0]
        for d in range(1, PIECES):
            mine += stats_all[level, d]

    ratio = mine[0:1, 0:1] / mine[1:2, 0:1]
    quotient[...] = jnp.broadcast_to(ratio, quotient.shape)
    row_ids = lax.broadcasted_iota(jnp.int32, (rows, width), 0) + z * rows
    column_ids = lax.broadcasted_iota(jnp.int32, (rows, width), 1)
    for j in range(PIECES):
        slot_width = width_of(group * 4 + j)
        keep = jnp.logical_and(row_ids < slot_width, column_ids < slot_width)
        live = lives[j, :rows, :width].astype(jnp.float32)
        value = jnp.where(keep, product[j] - ratio * live, 0.0)
        residual[j] = value.astype(residual.dtype)

    @pl.loop(0, units)
    def _(u):
        core_copy(0, u).wait_send()
        core_copy(1, u).wait_send()
        x_copy(u).wait_send()

    @pl.loop(0, units - 2)
    def _(i):
        z_copy(unit_of(i), z).wait_send()

    for p in range(PIECES):

        @pl.when(p * 4 + z != me)
        def _():
            live_copy(p, group).wait_send()

    for level in range(2):
        here = group if level == 0 else z
        for d in range(1, PIECES):
            stats_copy(level, (here + d) % PIECES, here).wait_send()


def kernel_shards(
    wavefunction, left_blocks, right_blocks, diagonal, target_sector, slot_sector, widths
):
    terms, _, width, _ = left_blocks.shape
    owners = slot_sector.shape[0]
    rows = width // PIECES
    groups = owners // PIECES
    capacity = (terms + groups) // groups
    units = 2 * PIECES
    tall = round_up(rows, 16)
    lanes = round_up(width, 128)
    block = (tall, round_up(2 * width, 128))
    vmem = pl.BlockSpec(memory_space=pltpu.VMEM)
    hbm = pl.BlockSpec(memory_space=pl.ANY)
    dma = pltpu.SemaphoreType.DMA
    wide = jnp.bfloat16
    residual, quotient = pl.pallas_call(
        fused_kernel,
        out_shape=(
            jax.ShapeDtypeStruct((PIECES, rows, width), jnp.bfloat16),
            jax.ShapeDtypeStruct((1, 1), jnp.float32),
        ),
        in_specs=[hbm] * 7,
        out_specs=(vmem, vmem),
        scratch_shapes=[
            pltpu.VMEM((1, owners), jnp.int32),
            pltpu.VMEM((owners, terms), jnp.int32),
            pltpu.VMEM((1, owners), jnp.int32),
            pltpu.VMEM((width, width), wide),
            pltpu.VMEM((8, 128), jnp.int32),
            pltpu.SMEM((8, 128), jnp.int32),
            pltpu.VMEM((terms, width, width), wide),
            pltpu.VMEM((terms, width, width), wide),
            pltpu.VMEM((capacity + 1, width, width), jnp.float32),
            pltpu.VMEM((4, units, *block), wide),
            pltpu.VMEM((2, units, *block), wide),
            pltpu.VMEM((units, *block), wide),
            pltpu.VMEM((PIECES, 2, *block), wide),
            pltpu.VMEM((PIECES, tall, lanes), wide),
            pltpu.VMEM((PIECES, tall, lanes), wide),
            pltpu.VMEM((rows, PIECES, width), jnp.float32),
            pltpu.VMEM((PIECES, rows, width), jnp.float32),
            pltpu.VMEM((2, 8, 128), jnp.float32),
            pltpu.VMEM((2, PIECES, 8, 128), jnp.float32),
            dma((4,)), dma, dma((terms,)), dma((terms,)), dma, dma,
            dma((2, units)), dma((2, units)), dma((units,)), dma((units,)),
            dma((units,)), dma((PIECES, 2)),
            dma((PIECES,)), dma((PIECES,)), dma((2, PIECES)), dma((2, PIECES)),
        ],
        compiler_params=pltpu.CompilerParams(
            collective_id=0, has_side_effects=True, vmem_limit_bytes=58 << 20
        ),
        name="fused",
    )(
        slot_sector[None], target_sector.T, widths[None], wavefunction,
        left_blocks[:, 0], right_blocks[:, 0], jnp.transpose(diagonal, (1, 0, 2)),
    )
    return residual, jnp.reshape(quotient, (1,))


def solution(mesh):
    in_specs = (
        P(("rep", "sec"), None, None),
        P(None, ("rep", "sec"), None, None),
        P(None, ("rep", "sec"), None, None),
        P(("rep", "sec"), None, None),
        P("rep", None),
        P("rep"),
        P("rep"),
    )
    out_specs = (P(("rep", "sec"), None, None), P("rep"))
    fast = mesh.shape["sec"] == PIECES * 4
    shards = kernel_shards if fast else gathered_shards
    return jax.shard_map(shards, mesh=mesh, in_specs=in_specs, out_specs=out_specs, check_vma=False)
```

```python
import functools

import jax
import jax.numpy as jnp
from jax import lax
from jax.experimental import pallas as pl
from jax.experimental.pallas import tpu as pltpu
from jax.sharding import PartitionSpec as P

PIECES = 4
MESH = pl.DeviceIdType.MESH


def earlier_same(labels):
    count = labels.shape[-1]
    same_label = labels[..., :, None] == labels[..., None, :]
    earlier = jnp.arange(count)[None, :] < jnp.arange(count)[:, None]
    return jnp.sum(jnp.logical_and(same_label, earlier).astype(jnp.int32), axis=-1)


def gathered_shards(wavefunction, left_blocks, right_blocks, diagonal, target_sector, slot_sector, widths):
    owners = lax.axis_size("sec")
    own_index = lax.axis_index("sec")
    term_count = left_blocks.shape[0]
    block_width = wavefunction.shape[1]
    piece_rows = block_width // PIECES
    groups = owners // PIECES
    capacity = (term_count + groups) // groups
    item_count = term_count + 1
    positions = jnp.arange(owners, dtype=jnp.int32)
    slot_of = jnp.zeros((owners,), jnp.int32).at[slot_sector].set(positions)
    targets = slot_of[target_sector[:, slot_sector]]
    live_width = widths[slot_sector]
    column_ids = jnp.arange(block_width, dtype=jnp.int32)
    own_keep = column_ids < live_width[own_index]
    live_block = wavefunction[0] * jnp.logical_and(own_keep[:, None], own_keep[None, :]).astype(
        wavefunction.dtype
    )
    item_slots = jnp.concatenate([jnp.reshape(own_index, (1,)), targets[:, own_index]])
    item_groups = item_slots // PIECES
    item_rank = earlier_same(item_groups)
    destination = jnp.arange(PIECES, dtype=jnp.int32)[None, :] * groups + item_groups[:, None]
    rank_grid = jnp.broadcast_to(item_rank[:, None], (item_count, PIECES))
    half_done = jnp.einsum(
        "tij,jk->tik", left_blocks[:, 0], live_block, preferred_element_type=jnp.float32
    ).astype(jnp.bfloat16)
    term_blocks = jnp.einsum(
        "tik,tlk->til", half_done, right_blocks[:, 0], preferred_element_type=jnp.float32
    ).astype(jnp.bfloat16)
    pieces = jnp.reshape(
        jnp.concatenate([live_block[None], term_blocks]),
        (item_count, PIECES, piece_rows, block_width),
    )
    outgoing = (
        jnp.zeros((owners, capacity, piece_rows, block_width), jnp.bfloat16)
        .at[destination, rank_grid]
        .set(pieces)
    )
    received = lax.all_to_all(outgoing, "sec", split_axis=0, concat_axis=0, tiled=True)
    my_piece = own_index // groups
    my_group = own_index % groups
    all_slots = jnp.concatenate([positions[:, None], jnp.transpose(targets)], axis=1)
    all_groups = all_slots // PIECES
    all_rank = earlier_same(all_groups)
    is_mine = all_groups == my_group
    rank_hit = jnp.logical_and(
        all_rank[:, :, None] == jnp.arange(capacity, dtype=jnp.int32)[None, None, :],
        is_mine[:, :, None],
    )
    place_hit = (
        (all_slots % PIECES)[:, :, None] == jnp.arange(PIECES, dtype=jnp.int32)[None, None, :]
    ).astype(jnp.float32)
    is_live = (jnp.arange(item_count) == 0)[None, :, None]
    live_weight = jnp.einsum(
        "smc,smp->scp", jnp.logical_and(rank_hit, is_live).astype(jnp.float32), place_hit
    )
    term_weight = jnp.einsum(
        "smc,smp->scp",
        jnp.logical_and(rank_hit, jnp.logical_not(is_live)).astype(jnp.float32),
        place_hit,
    )
    live_pieces = jnp.einsum(
        "scp,scab->pab",
        live_weight.astype(jnp.bfloat16),
        received,
        preferred_element_type=jnp.float32,
    )
    applied = jnp.einsum(
        "scp,scab->pab",
        term_weight.astype(jnp.bfloat16),
        received,
        preferred_element_type=jnp.float32,
    )
    my_slots = my_group * PIECES + jnp.arange(PIECES, dtype=jnp.int32)
    widths_here = live_width[my_slots]
    row_global = my_piece * piece_rows + jnp.arange(piece_rows, dtype=jnp.int32)
    keep_piece_rows = row_global[None, :] < widths_here[:, None]
    keep_piece_cols = column_ids[None, :] < widths_here[:, None]
    piece_box = jnp.logical_and(keep_piece_rows[:, :, None], keep_piece_cols[:, None, :]).astype(
        jnp.float32
    )
    product = diagonal * live_pieces + applied
    correlation_local = jnp.sum(live_pieces * product)
    correlation, squares = lax.psum((correlation_local, jnp.sum(live_pieces * live_pieces)), "sec")
    quotient = correlation / squares
    residual = ((product - quotient * live_pieces) * piece_box).astype(jnp.bfloat16)
    return (residual, jnp.reshape(quotient, (1,)))


def round_up(value, unit):
    return (value + unit - 1) // unit * unit


def to_column(row, count):
    wide = jnp.broadcast_to(row[:, :count], (count, count))
    eye = lax.broadcasted_iota(jnp.int32, (count, count), 0) == lax.broadcasted_iota(
        jnp.int32, (count, count), 1
    )
    return jnp.sum(jnp.where(eye, wide, 0.0), axis=1, keepdims=True)


def make_plan(slot_row, target_rows, width_row, me):
    owners, terms = target_rows.shape
    slot_column = to_column(slot_row, owners)
    at_owner = lax.broadcasted_iota(jnp.int32, (owners, 1), 0)
    sector = jnp.sum(jnp.where(at_owner == me, slot_column, 0.0), axis=0, keepdims=True)
    target = jnp.sum(
        jnp.where(at_owner.astype(jnp.float32) == sector, target_rows, 0.0), axis=0, keepdims=True
    )
    owner_ids = at_owner.astype(jnp.float32)
    slot = jnp.sum(jnp.where(slot_column == target, owner_ids, 0.0), axis=0, keepdims=True)
    column = to_column(slot, terms)
    term_row = lax.broadcasted_iota(jnp.int32, (terms, terms), 1)
    term_column = lax.broadcasted_iota(jnp.int32, (terms, terms), 0)
    ahead = jnp.logical_or(
        slot < column, jnp.logical_and(slot == column, term_row < term_column)
    )
    rank = jnp.sum(jnp.where(ahead, 1.0, 0.0), axis=1, keepdims=True)
    lanes = lax.broadcasted_iota(jnp.int32, (terms, 128), 1).astype(jnp.float32)
    term_ids = lax.broadcasted_iota(jnp.int32, (terms, 128), 0).astype(jnp.float32)
    order = jnp.sum(jnp.where(rank == lanes, term_ids, 0.0), axis=0, keepdims=True)
    start = jnp.sum(jnp.where(column < lanes, 1.0, 0.0), axis=0, keepdims=True)
    width_column = to_column(width_row, owners)
    widths = jnp.sum(
        jnp.where(owner_ids == slot_row, width_column, 0.0), axis=0, keepdims=True
    )
    return order, start, widths


def fused_kernel(
    slot_sector, target_sector, widths, wave, left, right, diagonal, residual, quotient,
    slot_vmem, target_vmem, width_vmem, wave_vmem, plan_vmem, plan, lbuf, rbuf, running,
    own, crecv, xrecv, zrecv, live_pieces, lives, diag_raw, product, stats, stats_all,
    small_sem, plan_sem, lsem, rsem, diag_sem, self_sem,
    csend_sem, crecv_sem, xsend_sem, xrecv_sem, zsend_sem, zrecv_sem,
    lsend_sem, lrecv_sem, ssend_sem, srecv_sem,
):
    rep = lax.axis_index("rep")
    me = lax.axis_index("sec")
    owners = slot_sector.shape[1]
    terms, width = lbuf.shape[0], lbuf.shape[1]
    groups = owners // PIECES
    capacity = (terms + groups) // groups
    z, x, c = me // 4, (me // 2) % 2, me % 2
    group = me % 4
    units = 2 * PIECES
    rows = width // PIECES
    main = width // 128 * 128
    rest = width - main
    far, near = (1 - x) * 2, x * 2

    small = [
        pltpu.make_async_copy(source, target, small_sem.at[i])
        for i, (source, target) in enumerate(
            (
                (wave.at[0], wave_vmem),
                (slot_sector, slot_vmem),
                (target_sector, target_vmem),
                (widths, width_vmem),
            )
        )
    ]
    for copy in small:
        copy.start()

    @pl.loop(0, terms)
    def _(t):
        pltpu.make_async_copy(left.at[t], lbuf.at[t], lsem.at[t]).start()

    @pl.loop(0, terms)
    def _(t):
        pltpu.make_async_copy(right.at[t], rbuf.at[t], rsem.at[t]).start()

    diag_copy = pltpu.make_async_copy(diagonal, diag_raw, diag_sem)
    diag_copy.start()

    barrier = pltpu.get_barrier_semaphore()
    for d in range(1, owners):
        pl.semaphore_signal(
            barrier, inc=1, device_id=(rep, me ^ d), device_id_type=MESH
        )

    for copy in small:
        copy.wait()
    order, start, slot_widths = make_plan(
        slot_vmem[...].astype(jnp.float32),
        target_vmem[...].astype(jnp.float32),
        width_vmem[...].astype(jnp.float32),
        me,
    )
    plan_vmem[0:1, :] = order.astype(jnp.int32)
    plan_vmem[1:2, :] = start.astype(jnp.int32)
    plan_copy = pltpu.make_async_copy(plan_vmem, plan, plan_sem)
    plan_copy.start()

    def width_of(slot):
        ids = lax.broadcasted_iota(jnp.int32, slot_widths.shape, 1)
        picked = jnp.sum(jnp.where(ids == slot, slot_widths, 0.0), axis=1, keepdims=True)
        return picked.astype(jnp.int32)

    own_width = width_of(me)
    row_ids = lax.broadcasted_iota(jnp.int32, (width, width), 0)
    column_ids = lax.broadcasted_iota(jnp.int32, (width, width), 1)
    keep = jnp.logical_and(row_ids < own_width, column_ids < own_width)
    live_wide = jnp.where(keep, wave_vmem[...].astype(jnp.float32), 0.0)
    live = live_wide.astype(jnp.bfloat16)
    for p in range(PIECES):
        piece = live_wide[p * rows : (p + 1) * rows].astype(jnp.bfloat16)
        live_pieces[p, :rows, :width] = piece

    def unit_of(i):
        hop = i // 2
        far_first = jnp.where(hop < 2, 2 + hop, 3 - hop)
        return (z ^ far_first) * 2 + i % 2

    def core_copy(which, u):
        return pltpu.make_async_remote_copy(
            src_ref=own.at[2 * which, u], dst_ref=crecv.at[which, u],
            send_sem=csend_sem.at[which, u], recv_sem=crecv_sem.at[which, u],
            device_id=(rep, near + z * 4 + (1 - c)), device_id_type=MESH,
        )

    def x_copy(u):
        return pltpu.make_async_remote_copy(
            src_ref=own.at[1, u], dst_ref=xrecv.at[u],
            send_sem=xsend_sem.at[u], recv_sem=xrecv_sem.at[u],
            device_id=(rep, z * 4 + far + c), device_id_type=MESH,
        )

    def z_copy(u, source_z):
        q = u % 2
        return pltpu.make_async_remote_copy(
            src_ref=own.at[3, u], dst_ref=zrecv.at[source_z, q],
            send_sem=zsend_sem.at[u], recv_sem=zrecv_sem.at[source_z, q],
            device_id=(rep, (u // 2) * 4 + group), device_id_type=MESH,
        )

    def live_copy(p, place):
        return pltpu.make_async_remote_copy(
            src_ref=live_pieces.at[p], dst_ref=lives.at[place],
            send_sem=lsend_sem.at[p], recv_sem=lrecv_sem.at[place],
            device_id=(rep, p * 4 + z), device_id_type=MESH,
        )

    def stats_copy(other, source):
        return pltpu.make_async_remote_copy(
            src_ref=stats, dst_ref=stats_all.at[source],
            send_sem=ssend_sem.at[other], recv_sem=srecv_sem.at[source],
            device_id=(rep, other), device_id_type=MESH,
        )

    batch = 4

    @pl.loop(0, terms // batch)
    def _(step):
        for b in range(batch):
            t = step * batch + b
            pltpu.make_async_copy(left.at[t], lbuf.at[t], lsem.at[t]).wait()
        for b in range(batch):
            t = step * batch + b
            half = jnp.dot(lbuf[t], live, preferred_element_type=jnp.float32)
            lbuf[t] = half.astype(jnp.bfloat16)

    pl.semaphore_wait(barrier, owners - 1)
    self_copy = pltpu.make_async_copy(live_pieces.at[z], lives.at[group], self_sem)
    for p in range(PIECES):

        @pl.when(p * 4 + z != me)
        def _():
            live_copy(p, group).start()

        @pl.when(p * 4 + z == me)
        def _():
            self_copy.start()

    running[0] = jnp.zeros((width, width), jnp.float32)
    plan_copy.wait()

    @pl.loop(0, terms)
    def _(t):
        pltpu.make_async_copy(right.at[t], rbuf.at[t], rsem.at[t]).wait()

    pad = jnp.zeros((rows, own.shape[-1] - 2 * width), jnp.float32)

    @pl.loop(0, groups)
    def _(k):
        target_group = jnp.where(k < 2, far, near) + jnp.where(k % 2 == 0, 1 - c, c)
        first = plan[1, target_group * PIECES]
        for i in range(capacity):
            t = jnp.clip(plan[0, jnp.clip(first + i, 0, terms - 1)], 0, terms - 1)
            term = lax.dot_general(
                lbuf[t], rbuf[t], (((1,), (1,)), ((), ())), preferred_element_type=jnp.float32
            )
            running[i + 1] = term if i == 0 else running[i] + term
        for q in range(2):
            ends = [
                jnp.clip(plan[1, target_group * PIECES + 2 * q + e] - first, 0, capacity)
                for e in range(3)
            ]
            for p in range(PIECES):
                at = slice(p * rows, (p + 1) * rows)
                low, middle, high = [running[end, at, :] for end in ends]
                even, odd = middle - low, high - middle
                packed = jnp.concatenate(
                    [even[:, :main], odd[:, :main], even[:, main:], odd[:, main:], pad], axis=1
                )
                own[k, 2 * p + q, :rows, :] = packed.astype(own.dtype)

        @pl.when(k % 2 == 0)
        def _():
            @pl.loop(0, units)
            def _(i):
                core_copy(k // 2, unit_of(i)).start()

        @pl.when(k == 1)
        def _():
            @pl.loop(0, units)
            def _(i):
                u = unit_of(i)
                core_copy(0, u).wait_recv()
                total = own[1, u].astype(jnp.float32) + crecv[0, u].astype(jnp.float32)
                own[1, u] = total.astype(own.dtype)
                x_copy(u).start()

    @pl.loop(0, units - 2)
    def _(i):
        u = unit_of(i)
        core_copy(1, u).wait_recv()
        x_copy(u).wait_recv()
        total = own[3, u].astype(jnp.float32) + crecv[1, u].astype(jnp.float32)
        total += xrecv[u].astype(jnp.float32)
        own[3, u] = total.astype(own.dtype)
        z_copy(u, z).start()

    for j in range(PIECES):
        source = group * 4 + j

        @pl.when(source != me)
        def _():
            live_copy(0, j).wait_recv()

        @pl.when(source == me)
        def _():
            self_copy.wait()

    diag_copy.wait()
    for j in range(PIECES):
        product[j] = diag_raw[:, j, :] * lives[j, :rows, :width].astype(jnp.float32)

    correlation = jnp.zeros((1, width), jnp.float32)
    squares = jnp.zeros((1, width), jnp.float32)
    for q in range(2):
        u = z * 2 + q
        core_copy(1, u).wait_recv()
        x_copy(u).wait_recv()
        total = own[3, u].astype(jnp.float32) + crecv[1, u].astype(jnp.float32)
        total += xrecv[u].astype(jnp.float32)
        for d in range(1, PIECES):
            source_z = (z + d) % PIECES
            z_copy(q, source_z).wait_recv()
            total += zrecv[source_z, q].astype(jnp.float32)
        total = total[:rows]
        tail = 2 * main
        for parity in range(2):
            j = 2 * q + parity
            applied = jnp.concatenate(
                [
                    total[:, parity * main : (parity + 1) * main],
                    total[:, tail + parity * rest : tail + (parity + 1) * rest],
                ],
                axis=1,
            )
            live = lives[j, :rows, :width].astype(jnp.float32)
            block = product[j] + applied
            product[j] = block
            correlation += jnp.sum(live * block, axis=0, keepdims=True)
            squares += jnp.sum(live * live, axis=0, keepdims=True)

    row_ids = lax.broadcasted_iota(jnp.int32, stats.shape, 0)
    mine = jnp.where(row_ids == 0, jnp.sum(correlation), jnp.sum(squares))
    stats[...] = mine
    stats_all[me] = mine
    for d in range(owners - 1, 0, -1):
        stats_copy(me ^ d, me).start()
    for d in range(1, owners):
        stats_copy(me, me ^ d).wait_recv()
    mine = stats_all[0]
    for d in range(1, owners):
        mine += stats_all[d]

    ratio = mine[0:1, 0:1] / mine[1:2, 0:1]
    quotient[...] = jnp.broadcast_to(ratio, quotient.shape)
    row_ids = lax.broadcasted_iota(jnp.int32, (rows, width), 0) + z * rows
    column_ids = lax.broadcasted_iota(jnp.int32, (rows, width), 1)
    for j in range(PIECES):
        slot_width = width_of(group * 4 + j)
        keep = jnp.logical_and(row_ids < slot_width, column_ids < slot_width)
        live = lives[j, :rows, :width].astype(jnp.float32)
        value = jnp.where(keep, product[j] - ratio * live, 0.0)
        residual[j] = value.astype(residual.dtype)

    @pl.loop(0, units)
    def _(u):
        core_copy(0, u).wait_send()
        core_copy(1, u).wait_send()
        x_copy(u).wait_send()

    @pl.loop(0, units - 2)
    def _(i):
        z_copy(unit_of(i), z).wait_send()

    for p in range(PIECES):

        @pl.when(p * 4 + z != me)
        def _():
            live_copy(p, group).wait_send()

    for d in range(1, owners):
        stats_copy(me ^ d, me).wait_send()


def kernel_shards(
    wavefunction, left_blocks, right_blocks, diagonal, target_sector, slot_sector, widths
):
    terms, _, width, _ = left_blocks.shape
    owners = slot_sector.shape[0]
    rows = width // PIECES
    groups = owners // PIECES
    capacity = (terms + groups) // groups
    units = 2 * PIECES
    tall = round_up(rows, 16)
    lanes = round_up(width, 128)
    block = (tall, round_up(2 * width, 128))
    vmem = pl.BlockSpec(memory_space=pltpu.VMEM)
    hbm = pl.BlockSpec(memory_space=pl.ANY)
    dma = pltpu.SemaphoreType.DMA
    wide = jnp.bfloat16
    residual, quotient = pl.pallas_call(
        fused_kernel,
        out_shape=(
            jax.ShapeDtypeStruct((PIECES, rows, width), jnp.bfloat16),
            jax.ShapeDtypeStruct((1, 1), jnp.float32),
        ),
        in_specs=[hbm] * 7,
        out_specs=(vmem, vmem),
        scratch_shapes=[
            pltpu.VMEM((1, owners), jnp.int32),
            pltpu.VMEM((owners, terms), jnp.int32),
            pltpu.VMEM((1, owners), jnp.int32),
            pltpu.VMEM((width, width), wide),
            pltpu.VMEM((8, 128), jnp.int32),
            pltpu.SMEM((8, 128), jnp.int32),
            pltpu.VMEM((terms, width, width), wide),
            pltpu.VMEM((terms, width, width), wide),
            pltpu.VMEM((capacity + 1, width, width), jnp.float32),
            pltpu.VMEM((4, units, *block), wide),
            pltpu.VMEM((2, units, *block), wide),
            pltpu.VMEM((units, *block), wide),
            pltpu.VMEM((PIECES, 2, *block), wide),
            pltpu.VMEM((PIECES, tall, lanes), wide),
            pltpu.VMEM((PIECES, tall, lanes), wide),
            pltpu.VMEM((rows, PIECES, width), jnp.float32),
            pltpu.VMEM((PIECES, rows, width), jnp.float32),
            pltpu.VMEM((8, 128), jnp.float32),
            pltpu.VMEM((owners, 8, 128), jnp.float32),
            dma((4,)), dma, dma((terms,)), dma((terms,)), dma, dma,
            dma((2, units)), dma((2, units)), dma((units,)), dma((units,)),
            dma((units,)), dma((PIECES, 2)),
            dma((PIECES,)), dma((PIECES,)), dma((owners,)), dma((owners,)),
        ],
        compiler_params=pltpu.CompilerParams(
            collective_id=0, has_side_effects=True, vmem_limit_bytes=58 << 20
        ),
        name="fused",
    )(
        slot_sector[None], target_sector.T, widths[None], wavefunction,
        left_blocks[:, 0], right_blocks[:, 0], jnp.transpose(diagonal, (1, 0, 2)),
    )
    return residual, jnp.reshape(quotient, (1,))


def solution(mesh):
    in_specs = (
        P(("rep", "sec"), None, None),
        P(None, ("rep", "sec"), None, None),
        P(None, ("rep", "sec"), None, None),
        P(("rep", "sec"), None, None),
        P("rep", None),
        P("rep"),
        P("rep"),
    )
    out_specs = (P(("rep", "sec"), None, None), P("rep"))
    fast = mesh.shape["sec"] == PIECES * 4
    shards = kernel_shards if fast else gathered_shards
    return jax.shard_map(shards, mesh=mesh, in_specs=in_specs, out_specs=out_specs, check_vma=False)
```

```python
import functools

import jax
import jax.numpy as jnp
from jax import lax
from jax.experimental import pallas as pl
from jax.experimental.pallas import tpu as pltpu
from jax.sharding import PartitionSpec as P

PIECES = 4
MESH = pl.DeviceIdType.MESH


def earlier_same(labels):
    count = labels.shape[-1]
    same_label = labels[..., :, None] == labels[..., None, :]
    earlier = jnp.arange(count)[None, :] < jnp.arange(count)[:, None]
    return jnp.sum(jnp.logical_and(same_label, earlier).astype(jnp.int32), axis=-1)


def gathered_shards(wavefunction, left_blocks, right_blocks, diagonal, target_sector, slot_sector, widths):
    owners = lax.axis_size("sec")
    own_index = lax.axis_index("sec")
    term_count = left_blocks.shape[0]
    block_width = wavefunction.shape[1]
    piece_rows = block_width // PIECES
    groups = owners // PIECES
    capacity = (term_count + groups) // groups
    item_count = term_count + 1
    positions = jnp.arange(owners, dtype=jnp.int32)
    slot_of = jnp.zeros((owners,), jnp.int32).at[slot_sector].set(positions)
    targets = slot_of[target_sector[:, slot_sector]]
    live_width = widths[slot_sector]
    column_ids = jnp.arange(block_width, dtype=jnp.int32)
    own_keep = column_ids < live_width[own_index]
    live_block = wavefunction[0] * jnp.logical_and(own_keep[:, None], own_keep[None, :]).astype(
        wavefunction.dtype
    )
    item_slots = jnp.concatenate([jnp.reshape(own_index, (1,)), targets[:, own_index]])
    item_groups = item_slots // PIECES
    item_rank = earlier_same(item_groups)
    destination = jnp.arange(PIECES, dtype=jnp.int32)[None, :] * groups + item_groups[:, None]
    rank_grid = jnp.broadcast_to(item_rank[:, None], (item_count, PIECES))
    half_done = jnp.einsum(
        "tij,jk->tik", left_blocks[:, 0], live_block, preferred_element_type=jnp.float32
    ).astype(jnp.bfloat16)
    term_blocks = jnp.einsum(
        "tik,tlk->til", half_done, right_blocks[:, 0], preferred_element_type=jnp.float32
    ).astype(jnp.bfloat16)
    pieces = jnp.reshape(
        jnp.concatenate([live_block[None], term_blocks]),
        (item_count, PIECES, piece_rows, block_width),
    )
    outgoing = (
        jnp.zeros((owners, capacity, piece_rows, block_width), jnp.bfloat16)
        .at[destination, rank_grid]
        .set(pieces)
    )
    received = lax.all_to_all(outgoing, "sec", split_axis=0, concat_axis=0, tiled=True)
    my_piece = own_index // groups
    my_group = own_index % groups
    all_slots = jnp.concatenate([positions[:, None], jnp.transpose(targets)], axis=1)
    all_groups = all_slots // PIECES
    all_rank = earlier_same(all_groups)
    is_mine = all_groups == my_group
    rank_hit = jnp.logical_and(
        all_rank[:, :, None] == jnp.arange(capacity, dtype=jnp.int32)[None, None, :],
        is_mine[:, :, None],
    )
    place_hit = (
        (all_slots % PIECES)[:, :, None] == jnp.arange(PIECES, dtype=jnp.int32)[None, None, :]
    ).astype(jnp.float32)
    is_live = (jnp.arange(item_count) == 0)[None, :, None]
    live_weight = jnp.einsum(
        "smc,smp->scp", jnp.logical_and(rank_hit, is_live).astype(jnp.float32), place_hit
    )
    term_weight = jnp.einsum(
        "smc,smp->scp",
        jnp.logical_and(rank_hit, jnp.logical_not(is_live)).astype(jnp.float32),
        place_hit,
    )
    live_pieces = jnp.einsum(
        "scp,scab->pab",
        live_weight.astype(jnp.bfloat16),
        received,
        preferred_element_type=jnp.float32,
    )
    applied = jnp.einsum(
        "scp,scab->pab",
        term_weight.astype(jnp.bfloat16),
        received,
        preferred_element_type=jnp.float32,
    )
    my_slots = my_group * PIECES + jnp.arange(PIECES, dtype=jnp.int32)
    widths_here = live_width[my_slots]
    row_global = my_piece * piece_rows + jnp.arange(piece_rows, dtype=jnp.int32)
    keep_piece_rows = row_global[None, :] < widths_here[:, None]
    keep_piece_cols = column_ids[None, :] < widths_here[:, None]
    piece_box = jnp.logical_and(keep_piece_rows[:, :, None], keep_piece_cols[:, None, :]).astype(
        jnp.float32
    )
    product = diagonal * live_pieces + applied
    correlation_local = jnp.sum(live_pieces * product)
    correlation, squares = lax.psum((correlation_local, jnp.sum(live_pieces * live_pieces)), "sec")
    quotient = correlation / squares
    residual = ((product - quotient * live_pieces) * piece_box).astype(jnp.bfloat16)
    return (residual, jnp.reshape(quotient, (1,)))


def round_up(value, unit):
    return (value + unit - 1) // unit * unit


def to_column(row, count):
    wide = jnp.broadcast_to(row[:, :count], (count, count))
    eye = lax.broadcasted_iota(jnp.int32, (count, count), 0) == lax.broadcasted_iota(
        jnp.int32, (count, count), 1
    )
    return jnp.sum(jnp.where(eye, wide, 0.0), axis=1, keepdims=True)


def make_plan(slot_row, target_rows, width_row, me):
    owners, terms = target_rows.shape
    slot_column = to_column(slot_row, owners)
    at_owner = lax.broadcasted_iota(jnp.int32, (owners, 1), 0)
    sector = jnp.sum(jnp.where(at_owner == me, slot_column, 0.0), axis=0, keepdims=True)
    target = jnp.sum(
        jnp.where(at_owner.astype(jnp.float32) == sector, target_rows, 0.0), axis=0, keepdims=True
    )
    owner_ids = at_owner.astype(jnp.float32)
    slot = jnp.sum(jnp.where(slot_column == target, owner_ids, 0.0), axis=0, keepdims=True)
    column = to_column(slot, terms)
    term_row = lax.broadcasted_iota(jnp.int32, (terms, terms), 1)
    term_column = lax.broadcasted_iota(jnp.int32, (terms, terms), 0)
    ahead = jnp.logical_or(
        slot < column, jnp.logical_and(slot == column, term_row < term_column)
    )
    rank = jnp.sum(jnp.where(ahead, 1.0, 0.0), axis=1, keepdims=True)
    lanes = lax.broadcasted_iota(jnp.int32, (terms, 128), 1).astype(jnp.float32)
    term_ids = lax.broadcasted_iota(jnp.int32, (terms, 128), 0).astype(jnp.float32)
    order = jnp.sum(jnp.where(rank == lanes, term_ids, 0.0), axis=0, keepdims=True)
    start = jnp.sum(jnp.where(column < lanes, 1.0, 0.0), axis=0, keepdims=True)
    width_column = to_column(width_row, owners)
    widths = jnp.sum(
        jnp.where(owner_ids == slot_row, width_column, 0.0), axis=0, keepdims=True
    )
    return order, start, widths


def fused_kernel(
    slot_sector, target_sector, widths, wave, left, right, diagonal, residual, quotient,
    slot_vmem, target_vmem, width_vmem, wave_vmem, plan_vmem, plan, lbuf, rbuf, running,
    own, crecv, xrecv, zrecv, live_pieces, lives, diag_raw, product, stats, stats_all,
    small_sem, plan_sem, lsem, rsem, diag_sem, self_sem,
    csend_sem, crecv_sem, xsend_sem, xrecv_sem, zsend_sem, zrecv_sem,
    lsend_sem, lrecv_sem, ssend_sem, srecv_sem,
):
    rep = lax.axis_index("rep")
    me = lax.axis_index("sec")
    owners = slot_sector.shape[1]
    terms, width = lbuf.shape[0], lbuf.shape[1]
    groups = owners // PIECES
    capacity = (terms + groups) // groups
    z, x, c = me // 4, (me // 2) % 2, me % 2
    group = me % 4
    units = 2 * PIECES
    rows = width // PIECES
    main = width // 128 * 128
    rest = width - main
    far, near = (1 - x) * 2, x * 2

    small = [
        pltpu.make_async_copy(source, target, small_sem.at[i])
        for i, (source, target) in enumerate(
            (
                (wave.at[0], wave_vmem),
                (slot_sector, slot_vmem),
                (target_sector, target_vmem),
                (widths, width_vmem),
            )
        )
    ]
    for copy in small:
        copy.start()

    @pl.loop(0, terms)
    def _(t):
        pltpu.make_async_copy(left.at[t], lbuf.at[t], lsem.at[t]).start()

    @pl.loop(0, terms)
    def _(t):
        pltpu.make_async_copy(right.at[t], rbuf.at[t], rsem.at[t]).start()

    diag_copy = pltpu.make_async_copy(diagonal, diag_raw, diag_sem)
    diag_copy.start()

    barrier = pltpu.get_barrier_semaphore()
    for d in range(1, owners):
        pl.semaphore_signal(
            barrier, inc=1, device_id=(rep, me ^ d), device_id_type=MESH
        )

    for copy in small:
        copy.wait()
    order, start, slot_widths = make_plan(
        slot_vmem[...].astype(jnp.float32),
        target_vmem[...].astype(jnp.float32),
        width_vmem[...].astype(jnp.float32),
        me,
    )
    plan_vmem[0:1, :] = order.astype(jnp.int32)
    plan_vmem[1:2, :] = start.astype(jnp.int32)
    plan_copy = pltpu.make_async_copy(plan_vmem, plan, plan_sem)
    plan_copy.start()

    def width_of(slot):
        ids = lax.broadcasted_iota(jnp.int32, slot_widths.shape, 1)
        picked = jnp.sum(jnp.where(ids == slot, slot_widths, 0.0), axis=1, keepdims=True)
        return picked.astype(jnp.int32)

    own_width = width_of(me)
    row_ids = lax.broadcasted_iota(jnp.int32, (width, width), 0)
    column_ids = lax.broadcasted_iota(jnp.int32, (width, width), 1)
    keep = jnp.logical_and(row_ids < own_width, column_ids < own_width)
    live_wide = jnp.where(keep, wave_vmem[...].astype(jnp.float32), 0.0)
    live = live_wide.astype(jnp.bfloat16)
    for p in range(PIECES):
        piece = live_wide[p * rows : (p + 1) * rows].astype(jnp.bfloat16)
        live_pieces[p, :rows, :width] = piece

    def unit_of(i):
        hop = i // 2
        away = jnp.where(hop == 0, 3, jnp.where(hop == 1, 1, jnp.where(hop == 2, 2, 0)))
        return (z ^ away) * 2 + i % 2

    def core_copy(which, u):
        return pltpu.make_async_remote_copy(
            src_ref=own.at[2 * which, u], dst_ref=crecv.at[which, u],
            send_sem=csend_sem.at[which, u], recv_sem=crecv_sem.at[which, u],
            device_id=(rep, near + z * 4 + (1 - c)), device_id_type=MESH,
        )

    def x_copy(u):
        return pltpu.make_async_remote_copy(
            src_ref=own.at[1, u], dst_ref=xrecv.at[u],
            send_sem=xsend_sem.at[u], recv_sem=xrecv_sem.at[u],
            device_id=(rep, z * 4 + far + c), device_id_type=MESH,
        )

    def z_copy(i):
        hop, q = i // 2, i % 2
        target = z ^ jnp.where(hop < 2, 1, 2)
        return pltpu.make_async_remote_copy(
            src_ref=own.at[3, unit_of(i)], dst_ref=zrecv.at[hop, q],
            send_sem=zsend_sem.at[hop, q], recv_sem=zrecv_sem.at[hop, q],
            device_id=(rep, target * 4 + group), device_id_type=MESH,
        )

    def live_copy(p, place):
        return pltpu.make_async_remote_copy(
            src_ref=live_pieces.at[p], dst_ref=lives.at[place],
            send_sem=lsend_sem.at[p], recv_sem=lrecv_sem.at[place],
            device_id=(rep, p * 4 + z), device_id_type=MESH,
        )

    def stats_copy(other, source):
        return pltpu.make_async_remote_copy(
            src_ref=stats, dst_ref=stats_all.at[source],
            send_sem=ssend_sem.at[other], recv_sem=srecv_sem.at[source],
            device_id=(rep, other), device_id_type=MESH,
        )

    batch = 4

    @pl.loop(0, terms // batch)
    def _(step):
        for b in range(batch):
            t = step * batch + b
            pltpu.make_async_copy(left.at[t], lbuf.at[t], lsem.at[t]).wait()
        for b in range(batch):
            t = step * batch + b
            half = jnp.dot(lbuf[t], live, preferred_element_type=jnp.float32)
            lbuf[t] = half.astype(jnp.bfloat16)

    pl.semaphore_wait(barrier, owners - 1)
    self_copy = pltpu.make_async_copy(live_pieces.at[z], lives.at[group], self_sem)
    for p in range(PIECES):

        @pl.when(p * 4 + z != me)
        def _():
            live_copy(p, group).start()

        @pl.when(p * 4 + z == me)
        def _():
            self_copy.start()

    running[0] = jnp.zeros((width, width), jnp.float32)
    plan_copy.wait()

    @pl.loop(0, terms)
    def _(t):
        pltpu.make_async_copy(right.at[t], rbuf.at[t], rsem.at[t]).wait()

    pad = jnp.zeros((rows, own.shape[-1] - 2 * width), jnp.float32)

    @pl.loop(0, groups)
    def _(k):
        target_group = jnp.where(k < 2, far, near) + jnp.where(k % 2 == 0, 1 - c, c)
        first = plan[1, target_group * PIECES]
        for i in range(capacity):
            t = jnp.clip(plan[0, jnp.clip(first + i, 0, terms - 1)], 0, terms - 1)
            term = lax.dot_general(
                lbuf[t], rbuf[t], (((1,), (1,)), ((), ())), preferred_element_type=jnp.float32
            )
            running[i + 1] = term if i == 0 else running[i] + term
        for q in range(2):
            ends = [
                jnp.clip(plan[1, target_group * PIECES + 2 * q + e] - first, 0, capacity)
                for e in range(3)
            ]
            for p in range(PIECES):
                at = slice(p * rows, (p + 1) * rows)
                low, middle, high = [running[end, at, :] for end in ends]
                even, odd = middle - low, high - middle
                packed = jnp.concatenate(
                    [even[:, :main], odd[:, :main], even[:, main:], odd[:, main:], pad], axis=1
                )
                own[k, 2 * p + q, :rows, :] = packed.astype(own.dtype)

        @pl.when(k % 2 == 0)
        def _():
            @pl.loop(0, units)
            def _(i):
                core_copy(k // 2, unit_of(i)).start()

        @pl.when(k == 1)
        def _():
            @pl.loop(0, units)
            def _(i):
                u = unit_of(i)
                core_copy(0, u).wait_recv()
                total = own[1, u].astype(jnp.float32) + crecv[0, u].astype(jnp.float32)
                own[1, u] = total.astype(own.dtype)
                x_copy(u).start()

    def near_total(u):
        core_copy(1, u).wait_recv()
        x_copy(u).wait_recv()
        total = own[3, u].astype(jnp.float32) + crecv[1, u].astype(jnp.float32)
        return total + xrecv[u].astype(jnp.float32)

    @pl.loop(0, 4)
    def _(i):
        u = unit_of(i)
        own[3, u] = near_total(u).astype(own.dtype)
        z_copy(i).start()

    @pl.loop(4, 6)
    def _(i):
        u = unit_of(i)
        total = near_total(u)
        z_copy(i - 4).wait_recv()
        total += zrecv[0, i - 4].astype(jnp.float32)
        own[3, u] = total.astype(own.dtype)
        z_copy(i).start()

    for j in range(PIECES):
        source = group * 4 + j

        @pl.when(source != me)
        def _():
            live_copy(0, j).wait_recv()

        @pl.when(source == me)
        def _():
            self_copy.wait()

    diag_copy.wait()
    for j in range(PIECES):
        product[j] = diag_raw[:, j, :] * lives[j, :rows, :width].astype(jnp.float32)

    correlation = jnp.zeros((1, width), jnp.float32)
    squares = jnp.zeros((1, width), jnp.float32)
    for q in range(2):
        u = z * 2 + q
        total = near_total(u)
        for hop in range(1, 3):
            z_copy(2 * hop + q).wait_recv()
            total += zrecv[hop, q].astype(jnp.float32)
        total = total[:rows]
        tail = 2 * main
        for parity in range(2):
            j = 2 * q + parity
            applied = jnp.concatenate(
                [
                    total[:, parity * main : (parity + 1) * main],
                    total[:, tail + parity * rest : tail + (parity + 1) * rest],
                ],
                axis=1,
            )
            live = lives[j, :rows, :width].astype(jnp.float32)
            block = product[j] + applied
            product[j] = block
            correlation += jnp.sum(live * block, axis=0, keepdims=True)
            squares += jnp.sum(live * live, axis=0, keepdims=True)

    row_ids = lax.broadcasted_iota(jnp.int32, stats.shape, 0)
    mine = jnp.where(row_ids == 0, jnp.sum(correlation), jnp.sum(squares))
    stats[...] = mine
    stats_all[me] = mine
    for d in range(owners - 1, 0, -1):
        stats_copy(me ^ d, me).start()
    for d in range(1, owners):
        stats_copy(me, me ^ d).wait_recv()
    mine = stats_all[0]
    for d in range(1, owners):
        mine += stats_all[d]

    ratio = mine[0:1, 0:1] / mine[1:2, 0:1]
    quotient[...] = jnp.broadcast_to(ratio, quotient.shape)
    row_ids = lax.broadcasted_iota(jnp.int32, (rows, width), 0) + z * rows
    column_ids = lax.broadcasted_iota(jnp.int32, (rows, width), 1)
    for j in range(PIECES):
        slot_width = width_of(group * 4 + j)
        keep = jnp.logical_and(row_ids < slot_width, column_ids < slot_width)
        live = lives[j, :rows, :width].astype(jnp.float32)
        value = jnp.where(keep, product[j] - ratio * live, 0.0)
        residual[j] = value.astype(residual.dtype)

    @pl.loop(0, units)
    def _(u):
        core_copy(0, u).wait_send()
        core_copy(1, u).wait_send()
        x_copy(u).wait_send()

    @pl.loop(0, units - 2)
    def _(i):
        z_copy(i).wait_send()

    for p in range(PIECES):

        @pl.when(p * 4 + z != me)
        def _():
            live_copy(p, group).wait_send()

    for d in range(1, owners):
        stats_copy(me ^ d, me).wait_send()


def kernel_shards(
    wavefunction, left_blocks, right_blocks, diagonal, target_sector, slot_sector, widths
):
    terms, _, width, _ = left_blocks.shape
    owners = slot_sector.shape[0]
    rows = width // PIECES
    groups = owners // PIECES
    capacity = (terms + groups) // groups
    units = 2 * PIECES
    tall = round_up(rows, 16)
    lanes = round_up(width, 128)
    block = (tall, round_up(2 * width, 128))
    vmem = pl.BlockSpec(memory_space=pltpu.VMEM)
    hbm = pl.BlockSpec(memory_space=pl.ANY)
    dma = pltpu.SemaphoreType.DMA
    wide = jnp.bfloat16
    residual, quotient = pl.pallas_call(
        fused_kernel,
        out_shape=(
            jax.ShapeDtypeStruct((PIECES, rows, width), jnp.bfloat16),
            jax.ShapeDtypeStruct((1, 1), jnp.float32),
        ),
        in_specs=[hbm] * 7,
        out_specs=(vmem, vmem),
        scratch_shapes=[
            pltpu.VMEM((1, owners), jnp.int32),
            pltpu.VMEM((owners, terms), jnp.int32),
            pltpu.VMEM((1, owners), jnp.int32),
            pltpu.VMEM((width, width), wide),
            pltpu.VMEM((8, 128), jnp.int32),
            pltpu.SMEM((8, 128), jnp.int32),
            pltpu.VMEM((terms, width, width), wide),
            pltpu.VMEM((terms, width, width), wide),
            pltpu.VMEM((capacity + 1, width, width), jnp.float32),
            pltpu.VMEM((4, units, *block), wide),
            pltpu.VMEM((2, units, *block), wide),
            pltpu.VMEM((units, *block), wide),
            pltpu.VMEM((3, 2, *block), wide),
            pltpu.VMEM((PIECES, tall, lanes), wide),
            pltpu.VMEM((PIECES, tall, lanes), wide),
            pltpu.VMEM((rows, PIECES, width), jnp.float32),
            pltpu.VMEM((PIECES, rows, width), jnp.float32),
            pltpu.VMEM((8, 128), jnp.float32),
            pltpu.VMEM((owners, 8, 128), jnp.float32),
            dma((4,)), dma, dma((terms,)), dma((terms,)), dma, dma,
            dma((2, units)), dma((2, units)), dma((units,)), dma((units,)),
            dma((3, 2)), dma((3, 2)),
            dma((PIECES,)), dma((PIECES,)), dma((owners,)), dma((owners,)),
        ],
        compiler_params=pltpu.CompilerParams(
            collective_id=0, has_side_effects=True, vmem_limit_bytes=58 << 20
        ),
        name="fused",
    )(
        slot_sector[None], target_sector.T, widths[None], wavefunction,
        left_blocks[:, 0], right_blocks[:, 0], jnp.transpose(diagonal, (1, 0, 2)),
    )
    return residual, jnp.reshape(quotient, (1,))


def solution(mesh):
    in_specs = (
        P(("rep", "sec"), None, None),
        P(None, ("rep", "sec"), None, None),
        P(None, ("rep", "sec"), None, None),
        P(("rep", "sec"), None, None),
        P("rep", None),
        P("rep"),
        P("rep"),
    )
    out_specs = (P(("rep", "sec"), None, None), P("rep"))
    fast = mesh.shape["sec"] == PIECES * 4
    shards = kernel_shards if fast else gathered_shards
    return jax.shard_map(shards, mesh=mesh, in_specs=in_specs, out_specs=out_specs, check_vma=False)
```
